256 devices in a mesh: ctx: 32 (over x, z_lo, core), head: 8 (over y, z_hi).
Axes of the slice: x: 4, y: 4, z: 8 (z_hi: 2, z_lo: 4; z = z_hi * 4 + z_lo), core: 2. Of those that a mesh axis runs over, the one named last changes fastest.
Arguments:
- queries: bfloat16 [8192, 64, 128], P('ctx', 'head'), may hold values from -24 to 24, as said below
- self_keys: bfloat16 [8192, 8, 128], P('ctx', 'head'), may hold values from -24 to 24, as said below
- self_values: bfloat16 [8192, 8, 128], P('ctx', 'head'), may hold values from -6 to 6
- image_keys: bfloat16 [2048, 8, 128], P(('ctx', 'head')), may hold values from -24 to 24, as said below
- image_values: bfloat16 [2048, 8, 128], P(('ctx', 'head')), may hold values from -6 to 6
- image_offsets: int32 [4], replicated, may hold values from 0 to 8063, as said below
- first_image: int32 [64], replicated, may hold values from 0 to 4, as said below
- block_mask: int32 [64, 64], replicated, may hold values from 0 to 1, as said below
Outputs:
- self_attention: bfloat16 [8192, 64, 128], P('ctx', 'head')
- cross_attention: bfloat16 [8192, 64, 128], P('ctx', 'head')
The draws below stay inside these ranges and needn't reach their ends.
Inputs may be any that keep to these rules, and one draw needn't show every extreme that they name: `queries`: within the stated range; both draws stay there. `self_keys`: within the stated range; both draws stay there. `image_keys`: within the stated range; both draws stay there. `image_offsets`: strictly increasing; the last image is inserted at 8063. first_image[b] is at most the number of images whose offset lies below (128 * (b + 1)); the last block's entry is 0 and the entry of block 62 is 4. block_mask[q, k] is 1 for k == q, 0 for k > q, and 0 or 1 below the diagonal.
All inputs are finite; a program needn't handle non-finite values.
Results may differ from the reference program's by a relative error of at most 0.0049.
Values may be sent and summed in bfloat16 or wider, within the bound.
A program may use at most 64 MiB of HBM per device.

```python
import math
import jax
import jax.numpy as jnp
from jax import lax

QH = 64
KV = 8
HD = 128
IMG_LEN = 512
IMAGES = 4
BLK = 128
TOKENS = 8192
NBLK = 64
IMG_ROWS = 2048


def offsets_from(key):
    spacing = (TOKENS - BLK) // IMAGES
    jitter = jax.random.randint(jax.random.fold_in(key, 201), (IMAGES,), 0, spacing)
    image_ids = jnp.arange(IMAGES, dtype=jnp.int32)
    offsets = image_ids * spacing + jitter
    offsets = jnp.where(image_ids == IMAGES - 1, TOKENS - BLK - 1, offsets)
    return offsets.astype(jnp.int32)


def draw_queries(key, part):
    key = jax.random.fold_in(key, 21)
    result = jax.random.normal(key, (TOKENS, QH, HD), jnp.float32)
    return jnp.clip(result, -24.0, 24.0).astype(jnp.bfloat16)


def draw_self_keys(key, part):
    key = jax.random.fold_in(key, 22)
    scale_key, value_key = jax.random.split(key)
    row_scale = jnp.exp(jax.random.uniform(scale_key, (TOKENS, 1, 1), jnp.float32, math.log(0.3), math.log(3.0)))
    result = jax.random.normal(value_key, (TOKENS, KV, HD), jnp.float32) * row_scale
    return jnp.clip(result, -24.0, 24.0).astype(jnp.bfloat16)


def draw_image_keys(key, part):
    key = jax.random.fold_in(key, 23)
    scale_key, value_key = jax.random.split(key)
    row_scale = jnp.exp(jax.random.uniform(scale_key, (IMG_ROWS, 1, 1), jnp.float32, math.log(0.3), math.log(3.0)))
    result = jax.random.normal(value_key, (IMG_ROWS, KV, HD), jnp.float32) * row_scale
    return jnp.clip(result, -24.0, 24.0).astype(jnp.bfloat16)


def draw_image_offsets(key, part):
    offsets = offsets_from(key)
    return offsets


def draw_first_image(key, part):
    offsets = offsets_from(key)
    key = jax.random.fold_in(key, 32)
    block_ends = (jnp.arange(NBLK, dtype=jnp.int32) + 1) * BLK
    seen_count = jnp.sum((offsets[None, :] < block_ends[:, None]).astype(jnp.int32), axis=1)
    first = jax.random.randint(key, (NBLK,), 0, seen_count + 1)
    first = first.at[NBLK - 2].set(IMAGES)
    first = first.at[NBLK - 1].set(0)
    return first.astype(jnp.int32)


def draw_block_mask(key, part):
    key = jax.random.fold_in(key, 33)
    coins = jax.random.randint(key, (NBLK, NBLK), 0, 2)
    block_ids = jnp.arange(NBLK, dtype=jnp.int32)
    lower = block_ids[:, None] > block_ids[None, :]
    result = jnp.where(lower, coins, 0)
    result = jnp.where(block_ids[:, None] == block_ids[None, :], 1, result)
    return result.astype(jnp.int32)


def levels(key, extent, cuts, smallest, largest):
    loudness = 1.0
    for dim, parts in cuts:
        steps = jax.random.uniform(jax.random.fold_in(jax.random.fold_in(key, 6), dim), (parts,), jnp.float32, smallest / len(cuts), largest / len(cuts))
        loudness = loudness * jnp.repeat(jnp.exp(steps), extent[dim] // parts).reshape((-1,) + (1,) * (len(extent) - 1 - dim))
    return loudness


def gaussian(stream_key, dims, spread, most, cuts=(), held_as=jnp.bfloat16):
    loudness = levels(stream_key, dims, cuts, -0.22, 0.18) if cuts else 1.0
    values = jax.random.normal(stream_key, dims, jnp.float32) * spread * loudness
    return jnp.minimum(jnp.maximum(values, -most), most).astype(held_as)


def setup_inputs(seed: int = 0) -> dict:
    key_list = jax.random.split(jax.random.key(seed), 9)
    return {
        "queries": draw_queries(jax.random.fold_in(key_list[8], 71), 0),
        "self_keys": draw_self_keys(jax.random.fold_in(key_list[8], 71), 0),
        "self_values": gaussian(key_list[2], (TOKENS, KV, HD), 1.0, 6.0, ((0, 32), (1, 8))),
        "image_keys": draw_image_keys(jax.random.fold_in(key_list[8], 71), 0),
        "image_values": gaussian(key_list[4], (IMG_ROWS, KV, HD), 1.0, 6.0, ((0, 256),)),
        "image_offsets": draw_image_offsets(jax.random.fold_in(key_list[8], 71), 0),
        "first_image": draw_first_image(jax.random.fold_in(key_list[8], 71), 0),
        "block_mask": draw_block_mask(jax.random.fold_in(key_list[8], 71), 0),
    }


masked_score = -1e+30

def attend(head_queries, key_rows, value_rows, visible):
    scores = jnp.einsum('qgd,sd->gqs', head_queries, key_rows) / math.sqrt(HD)
    scores = jnp.where(visible[None], scores, masked_score)
    row_max = lax.optimization_barrier(jnp.max(scores, axis=-1, keepdims=True))
    weights = jnp.where(visible[None], jnp.exp(scores - row_max), 0.0)
    row_total = lax.optimization_barrier(jnp.sum(weights, axis=-1))
    rounded = lax.optimization_barrier(weights.astype(jnp.bfloat16)).astype(jnp.float32)
    weighted = jnp.einsum('gqs,sd->gqd', rounded, value_rows)
    return (weighted, row_total)

def reference(queries, self_keys, self_values, image_keys, image_values, image_offsets, first_image, block_mask):
    group_size = QH // KV
    key_pos = jnp.arange(TOKENS, dtype=jnp.int32)
    key_block = key_pos // BLK
    image_index = jnp.arange(IMG_ROWS, dtype=jnp.int32) // IMG_LEN
    image_start = image_offsets[image_index]
    keys_all = self_keys.astype(jnp.float32)
    values_all = self_values.astype(jnp.float32)
    image_kf = image_keys.astype(jnp.float32)
    image_vf = image_values.astype(jnp.float32)

    def per_block(block_number):
        query_rows = lax.dynamic_slice_in_dim(queries, block_number * BLK, BLK, 0).astype(jnp.float32)
        query_rows = query_rows.reshape(BLK, KV, group_size, HD)
        positions = block_number * BLK + jnp.arange(BLK, dtype=jnp.int32)
        mask_row = block_mask[block_number][key_block]
        earlier = (key_block[None, :] < block_number) & (mask_row[None, :] == 1)
        inside = (key_block[None, :] == block_number) & (key_pos[None, :] <= positions[:, None])
        self_visible = earlier | inside
        image_visible = (image_index[None, :] >= first_image[block_number]) & (image_start[None, :] <= positions[:, None])

        def per_head(head_number):
            head_queries = query_rows[:, head_number]
            weighted, row_total = attend(head_queries, keys_all[:, head_number], values_all[:, head_number], self_visible)
            self_part = weighted / row_total[..., None]
            weighted, row_total = attend(head_queries, image_kf[:, head_number], image_vf[:, head_number], image_visible)
            seen = row_total > 0
            cross_part = jnp.where(seen[..., None], weighted / jnp.where(seen, row_total, 1.0)[..., None], 0.0)
            return (self_part, cross_part)
        self_heads, cross_heads = lax.map(per_head, jnp.arange(KV, dtype=jnp.int32))
        self_heads = self_heads.transpose(2, 0, 1, 3).reshape(BLK, QH, HD).astype(jnp.bfloat16)
        cross_heads = cross_heads.transpose(2, 0, 1, 3).reshape(BLK, QH, HD).astype(jnp.bfloat16)
        return (self_heads, cross_heads)
    self_blocks, cross_blocks = lax.map(per_block, jnp.arange(NBLK, dtype=jnp.int32))
    return (self_blocks.reshape(TOKENS, QH, HD), cross_blocks.reshape(TOKENS, QH, HD))
```

```python
import functools
import math

import jax
import jax.numpy as jnp
from jax import lax
from jax.experimental import pallas as pl
from jax.experimental.pallas import tpu as pltpu
from jax.sharding import PartitionSpec as P

MESH = pl.DeviceIdType.MESH
BF16 = jnp.bfloat16
F32 = jnp.float32

HEADS = 8
XS, ZS = 4, 4
BLK = 128
GROUP = 8
ROWS = BLK * GROUP
IMAGES = 4
IMG_LEN = 512
TILE = 128
SPAN = 8
LOG2E = 1.4426950408889634
HIDDEN = -1e30
FLOOR = -1e28


def gather_kernel(
    k_ref, v_ref, ik_ref, iv_ref, kv, img,
    own, own_img, outbox, inbox,
    piece_s, piece_r, zs, zr, xs, xr, rs, rr, sibs, sibr, ixs, ixr, izs, izr, isibs, isibr, keep,
):
    c = lax.axis_index("ctx")
    h = lax.axis_index("head")
    x, z, a = c // 8, (c // 2) % 4, c % 2
    left, right, far = (x + 3) % 4, (x + 1) % 4, (x + 2) % 4
    order = (z, z + 1 - 2 * (z % 2), 2 - z // 2, 3 - 3 * (z // 2))
    inner = z * (3 - z) > 0
    near, beyond = 3 - z, 3 * (z - 1)

    def ctx(x_, z_, a_):
        return x_ * 8 + z_ * 2 + a_

    def ks(x_, z_, a_):
        return a_ * 16 + x_ * 4 + z_

    def si(x_, z_, a_):
        return a_ * 16 + z_ * 4 + x_

    def rcopy(src, dst, ssem, rsem, to_ctx, to_head):
        return pltpu.make_async_remote_copy(
            src_ref=src, dst_ref=dst, send_sem=ssem, recv_sem=rsem,
            device_id=(to_ctx, to_head), device_id_type=MESH,
        )

    pending = []

    def send(src, dst, ssem, rsem, to_ctx, to_head, when=None):
        def go():
            rcopy(src, dst, ssem, rsem, to_ctx, to_head).start()

        def done():
            rcopy(src, dst, ssem, rsem, to_ctx, to_head).wait_send()

        if when is None:
            go()
        else:
            pl.when(when)(go)
        pending.append((when, done))

    def arrived(dst, rsem):
        rcopy(dst, dst, rsem, rsem, ctx(x, z, 1 - a), h).wait_recv()

    barrier = pltpu.get_barrier_semaphore()

    def greet(to_ctx, to_head):
        pl.semaphore_signal(barrier, inc=1, device_id=(to_ctx, to_head), device_id_type=MESH)

    greet(ctx(x, z, 1 - a), h)
    for x_ in (left, right, far):
        greet(ctx(x_, z, a), h)
    for d in range(1, HEADS):
        greet(c, (h + d) % HEADS)

    @pl.when(z > 0)
    def _():
        greet(ctx(x, z - 1, a), h)

    @pl.when(z < 3)
    def _():
        greet(ctx(x, z + 1, a), h)

    both = jnp.concatenate([ik_ref[...].astype(F32), iv_ref[...].astype(F32)], axis=0)
    outbox[...] = jnp.swapaxes(both, 0, 1).astype(BF16)
    own[:256] = k_ref[...]
    own[256:] = v_ref[...]
    keep_own = pltpu.make_async_copy(own, kv.at[ks(x, z, a)], keep.at[0])
    keep_own.start()

    pl.semaphore_wait(barrier, 12 + (z + 3) // 4 - z // 3)

    for d in range(1, HEADS):
        to = (h + d) % HEADS
        send(outbox.at[to], inbox.at[d], piece_s.at[d], piece_r.at[d], c, to)

    def own_column(i):
        s = ks(x, order[i], a)
        src = own if i == 0 else kv.at[s]
        send(src, kv.at[s], xs.at[0, i], xr.at[0, i], ctx(right, z, a), h)
        send(src, kv.at[s], xs.at[1, i], xr.at[1, i], ctx(left, z, a), h)
        share(0, i)

    def share(kind, i):
        s = ks((x, left, right, far)[kind], order[i], a)
        src = own if (kind, i) == (0, 0) else kv.at[s]
        send(src, kv.at[s], sibs.at[kind, i], sibr.at[kind, i], ctx(x, z, 1 - a), h)

    def column(i):
        s = ks(x, order[i], a)
        arrived(kv.at[s], zr.at[order[i]])
        to = near if i == 1 else beyond
        send(kv.at[s], kv.at[s], zs.at[i + 1], zr.at[order[i]], ctx(x, to, a), h, inner)
        own_column(i)

    def from_left(i):
        s = ks(left, order[i], a)
        arrived(kv.at[s], xr.at[0, i])
        if i < 2:
            send(kv.at[s], kv.at[s], rs.at[i], rr.at[i], ctx(right, z, a), h)
        share(1, i)

    def from_right(i):
        s = ks(right, order[i], a)
        arrived(kv.at[s], xr.at[1, i])
        if i >= 2:
            send(kv.at[s], kv.at[s], rs.at[i], rr.at[i], ctx(left, z, a), h)
        share(2, i)

    def from_far(i):
        s = ks(far, order[i], a)
        arrived(kv.at[s], rr.at[i])
        share(3, i)

    def image_line(i):
        part = img.at[pl.ds(si(0, order[i], a), 4)]
        send(part, part, isibs.at[i], isibr.at[i], ctx(x, z, 1 - a), h)
        return part

    def image_arrived(i):
        part = img.at[pl.ds(si(0, order[i], a), 4)]
        arrived(part, izr.at[order[i]])
        to = near if i == 1 else beyond
        send(part, part, izs.at[i + 1], izr.at[order[i]], ctx(x, to, a), h, inner)
        image_line(i)

    s = ks(x, z, a)
    send(own, kv.at[s], zs.at[0], zr.at[z], ctx(x, z + 1, a), h, z < 3)
    send(own, kv.at[s], zs.at[1], zr.at[z], ctx(x, z - 1, a), h, z > 0)
    own_column(0)

    inbox[0] = outbox[h]
    for d in range(1, HEADS):
        arrived(inbox.at[d], piece_r.at[d])
    rows = inbox[...].astype(F32)
    si_mine = si(x, z, a)
    own_img[:64] = rows[:, :8, :].reshape(64, 128).astype(BF16)
    own_img[64:] = rows[:, 8:, :].reshape(64, 128).astype(BF16)
    keep_img = pltpu.make_async_copy(own_img, img.at[si_mine], keep.at[1])
    keep_img.start()
    for d, x_ in ((1, right), (2, far), (3, left)):
        send(own_img, img.at[si_mine], ixs.at[d], ixr.at[d], ctx(x_, z, a), h)

    column(1)
    from_left(0)
    from_right(0)
    for d, x_ in ((1, left), (2, far), (3, right)):
        arrived(img.at[si(x_, z, a)], ixr.at[d])
    keep_img.wait()
    part = image_line(0)
    send(part, part, izs.at[0], izr.at[z], ctx(x, z + 1, a), h, z < 3)
    send(part, part, izs.at[1], izr.at[z], ctx(x, z - 1, a), h, z > 0)
    column(2)
    from_left(1)
    from_right(1)
    column(3)
    image_arrived(1)
    from_far(0)
    from_right(2)
    from_left(2)
    image_arrived(2)
    from_right(3)
    from_far(1)
    image_arrived(3)
    from_far(2)
    from_left(3)
    from_far(3)

    for kind in range(4):
        for i in range(4):
            s = ks((x, left, right, far)[kind], order[i], 1 - a)
            arrived(kv.at[s], sibr.at[kind, i])
    for i in range(4):
        first = si(0, order[i], 1 - a)
        arrived(img.at[pl.ds(first, 4)], isibr.at[i])
    keep_own.wait()
    for when, done in pending:
        if when is None:
            done()
        else:
            pl.when(when)(done)


def attend_kernel(
    offsets_ref, first_ref, mask_ref, q_ref, kv_ref, img_ref, self_ref, cross_ref,
    keys, vals, acc, top, bias, seen,
):
    c = lax.axis_index("ctx")
    scale = LOG2E / math.sqrt(128.0)
    vals[:, 128:] = jnp.ones((SPAN * BLK, 128), BF16)

    def reset():
        top[...] = jnp.full_like(top, FLOOR)
        acc[...] = jnp.zeros_like(acc)

    def step(i, extra):
        for r in range(ROWS // TILE):
            here = pl.ds(r * TILE, TILE)
            q = q_ref[pl.ds(i * ROWS + r * TILE, TILE), :]
            scores = lax.dot_general(
                q, keys[...], (((1,), (1,)), ((), ())), preferred_element_type=F32
            )
            scores = scores + extra(r)
            old = top[here, :]
            new = jnp.maximum(old, jnp.max(scores, axis=1, keepdims=True))
            top[here, :] = new
            weights = jnp.exp2((scores - new[:, :1]) * scale).astype(BF16)
            shrink = jnp.exp2((old - new) * scale)
            shrink = jnp.concatenate([shrink, shrink], axis=1)
            acc[here, :] = acc[here, :] * shrink + jnp.dot(
                weights, vals[...], preferred_element_type=F32
            )

    def result():
        total = acc[:, 128:]
        good = total > 0.0
        return jnp.where(good, acc[:, :128] / jnp.where(good, total, 1.0), 0.0).astype(BF16)

    def place(b):
        dev = b // 2
        return (dev % 2) * 16 + (dev // 8) * 4 + (dev // 2) % 4, (b % 2) * BLK

    for i in range(2):
        qb = 2 * c + i
        seen[0] = qb

        def collect(b, n):
            vis = mask_ref[qb, b]
            seen[n] = b
            return n + vis

        count = lax.fori_loop(0, qb, collect, jnp.int32(1))
        reset()

        def load(t, b):
            s, half = place(b)
            half = pl.multiple_of(half, BLK)
            keys[t * BLK:(t + 1) * BLK, :] = kv_ref[s, pl.ds(half, BLK), :]
            vals[t * BLK:(t + 1) * BLK, :128] = kv_ref[s, pl.ds(256 + half, BLK), :]

        def span(j, _):
            for t in range(SPAN):
                n = j * SPAN + t
                live = n < count
                load(t, jnp.where(live, seen[jnp.where(live, n, 0)], qb))
                bias[:, t * BLK:(t + 1) * BLK] = jnp.full(
                    (1, BLK), jnp.where(live, 0.0, HIDDEN), F32
                )

            @pl.when(j == 0)
            def _():
                def extra(r):
                    per = TILE // GROUP
                    at = lax.broadcasted_iota(jnp.int32, (TILE, BLK), 0) // GROUP + r * per
                    key = lax.broadcasted_iota(jnp.int32, (TILE, BLK), 1)
                    tri = jnp.where(key <= at, 0.0, HIDDEN)
                    rest = jnp.broadcast_to(bias[:, BLK:], (TILE, (SPAN - 1) * BLK))
                    return jnp.concatenate([tri, rest], axis=1)

                step(i, extra)

            @pl.when(j > 0)
            def _():
                step(i, lambda r: bias[...])

            return 0

        lax.fori_loop(0, (count + SPAN - 1) // SPAN, span, 0)
        self_ref[i * ROWS:(i + 1) * ROWS, :] = result()

        reset()
        for pair in range(IMAGES // 2):
            m0 = 2 * pair
            last = qb * BLK + BLK - 1

            def vis(m):
                return (m >= first_ref[qb]) & (offsets_ref[m] <= last)

            @pl.when(vis(m0) | vis(m0 + 1))
            def _():
                for m in (m0, m0 + 1):
                    for d in range(8):
                        s = (d % 2) * 16 + (d // 2) * 4 + m
                        row = (m - m0) * IMG_LEN + d * 64
                        keys[row:row + 64, :] = img_ref[s, :64, :]
                        vals[row:row + 64, :128] = img_ref[s, 64:, :]

                def extra(r):
                    per = TILE // GROUP
                    at = (
                        lax.broadcasted_iota(jnp.int32, (TILE, IMG_LEN), 0) // GROUP
                        + (r * per + qb * BLK)
                    )
                    parts = []
                    for m in (m0, m0 + 1):
                        lowest = jnp.where(m >= first_ref[qb], offsets_ref[m], 1 << 30)
                        parts.append(jnp.where(at >= lowest, 0.0, HIDDEN))
                    return jnp.concatenate(parts, axis=1)

                step(i, extra)

        cross_ref[i * ROWS:(i + 1) * ROWS, :] = result()


def per_device(q, k, v, ik, iv, offsets, first, mask):
    vmem = pl.BlockSpec(memory_space=pltpu.VMEM)
    smem = pl.BlockSpec(memory_space=pltpu.SMEM)
    hbm = pl.BlockSpec(memory_space=pl.ANY)
    dma = pltpu.SemaphoreType.DMA
    kv, img = pl.pallas_call(
        gather_kernel,
        out_shape=(
            jax.ShapeDtypeStruct((32, 512, 128), BF16),
            jax.ShapeDtypeStruct((32, 128, 128), BF16),
        ),
        in_specs=[vmem] * 4,
        out_specs=(hbm, hbm),
        scratch_shapes=[
            pltpu.VMEM((512, 128), BF16),
            pltpu.VMEM((128, 128), BF16),
            pltpu.VMEM((8, 16, 128), BF16),
            pltpu.VMEM((8, 16, 128), BF16),
            dma((8,)), dma((8,)),
            dma((5,)), dma((4,)),
            dma((2, 4)), dma((2, 4)),
            dma((4,)), dma((4,)),
            dma((4, 4)), dma((4, 4)),
            dma((4,)), dma((4,)),
            dma((5,)), dma((4,)),
            dma((4,)), dma((4,)),
            dma((2,)),
        ],
        compiler_params=pltpu.CompilerParams(
            collective_id=0, has_side_effects=True, vmem_limit_bytes=24 * 2**20
        ),
    )(k.reshape(-1, 128), v.reshape(-1, 128), ik, iv)

    n = q.shape[0] * q.shape[1]
    self_out, cross_out = pl.pallas_call(
        attend_kernel,
        out_shape=(jax.ShapeDtypeStruct((n, 128), BF16),) * 2,
        in_specs=[smem] * 3 + [vmem] * 3,
        out_specs=(vmem, vmem),
        scratch_shapes=[
            pltpu.VMEM((SPAN * BLK, 128), BF16),
            pltpu.VMEM((SPAN * BLK, 256), BF16),
            pltpu.VMEM((ROWS, 256), F32),
            pltpu.VMEM((ROWS, 128), F32),
            pltpu.VMEM((1, SPAN * BLK), F32),
            pltpu.SMEM((128,), jnp.int32),
        ],
        compiler_params=pltpu.CompilerParams(vmem_limit_bytes=40 * 2**20),
    )(offsets, first, mask, q.reshape(n, 128), kv, img)
    return self_out.reshape(q.shape), cross_out.reshape(q.shape)


def solution(mesh):
    return jax.shard_map(
        per_device,
        mesh=mesh,
        in_specs=(
            P("ctx", "head", None),
            P("ctx", "head", None),
            P("ctx", "head", None),
            P(("ctx", "head"), None, None),
            P(("ctx", "head"), None, None),
            P(),
            P(),
            P(),
        ),
        out_specs=(P("ctx", "head", None), P("ctx", "head", None)),
        check_vma=False,
    )
```

```python
import functools
import math

import jax
import jax.numpy as jnp
from jax import lax
from jax.experimental import pallas as pl
from jax.experimental.pallas import tpu as pltpu
from jax.sharding import PartitionSpec as P

MESH = pl.DeviceIdType.MESH
BF16 = jnp.bfloat16
F32 = jnp.float32

HEADS = 8
XS, ZS = 4, 4
BLK = 128
GROUP = 8
ROWS = BLK * GROUP
IMAGES = 4
IMG_LEN = 512
TILE = 128
SPAN = 8
LATER = ((2, 1), (3, 1))
LAST = 31
LOG2E = 1.4426950408889634
HIDDEN = -1e30
FLOOR = -1e28


def soft_step(q_ref, keys, vals, acc, top, first_row, extra):
    scale = LOG2E / math.sqrt(128.0)
    for r in range(ROWS // TILE):
        here = pl.ds(first_row + r * TILE, TILE)
        scores = lax.dot_general(
            q_ref[here, :], keys[...], (((1,), (1,)), ((), ())), preferred_element_type=F32
        )
        scores = scores + extra(r)
        old = top[here, :]
        new = jnp.maximum(old, jnp.max(scores, axis=1, keepdims=True))
        top[here, :] = new
        weights = jnp.exp2((scores - new[:, :1]) * scale).astype(BF16)
        shrink = jnp.exp2((old - new) * scale)
        shrink = jnp.concatenate([shrink, shrink], axis=1)
        acc[here, :] = acc[here, :] * shrink + jnp.dot(
            weights, vals[...], preferred_element_type=F32
        )


def gather_kernel(
    k_hbm, v_hbm, ik_hbm, iv_hbm, q_hbm, mask_hbm, kv, img, acc, top,
    own, own_img, outbox, inbox, ik, iv, q, mask, keys, vals, bias,
    piece_s, piece_r, zs, zr, xs, xr, rs, rr, sibs, sibr, ixs, ixr, izs, izr, isibs, isibr, last_s, last_r, keep,
):
    c = lax.axis_index("ctx")
    h = lax.axis_index("head")
    x, z, a = c // 8, (c // 2) % 4, c % 2
    left, right, far = (x + 3) % 4, (x + 1) % 4, (x + 2) % 4
    order = (z, z + 1 - 2 * (z % 2), 2 - z // 2, 3 - 3 * (z // 2))
    final = (c // 24) * (31 - c) > 0

    def ctx(x_, z_, a_):
        return x_ * 8 + z_ * 2 + a_

    def ks(x_, z_, a_):
        return a_ * 16 + x_ * 4 + z_

    def si(x_, z_, a_):
        return a_ * 16 + z_ * 4 + x_

    def rcopy(src, dst, ssem, rsem, to_ctx, to_head):
        return pltpu.make_async_remote_copy(
            src_ref=src, dst_ref=dst, send_sem=ssem, recv_sem=rsem,
            device_id=(to_ctx, to_head), device_id_type=MESH,
        )

    pending = []

    def run(when, go):
        if when is None:
            go()
        else:
            pl.when(when)(go)

    def send(src, dst, ssem, rsem, to_ctx, to_head, when=None):
        run(when, lambda: rcopy(src, dst, ssem, rsem, to_ctx, to_head).start())
        pending.append(
            (when, lambda: rcopy(src, dst, ssem, rsem, to_ctx, to_head).wait_send())
        )

    def arrived(dst, rsem, when=None):
        run(when, lambda: rcopy(dst, dst, rsem, rsem, ctx(x, z, 1 - a), h).wait_recv())

    loads = [
        pltpu.make_async_copy(src, dst, keep.at[2 + n])
        for n, (src, dst) in enumerate((
            (k_hbm, own.at[pl.ds(0, 256)]), (v_hbm, own.at[pl.ds(256, 256)]),
            (ik_hbm, ik), (iv_hbm, iv), (q_hbm, q), (mask_hbm, mask),
        ))
    ]
    for load in loads:
        load.start()

    barrier = pltpu.get_barrier_semaphore()

    def greet(to_ctx, to_head):
        pl.semaphore_signal(barrier, inc=1, device_id=(to_ctx, to_head), device_id_type=MESH)

    for d in range(1, HEADS):
        greet(c, (h + d) % HEADS)
    greet(ctx(x, z, 1 - a), h)
    for x_ in (left, right, far):
        greet(ctx(x_, z, a), h)
    for dz in range(1, 4):
        greet(ctx(x, (z + dz) % 4, a), h)
    apart = (c // 24) * (1 - c // 29) * (1 - a)
    pl.when(apart > 0)(lambda: greet(LAST, h))

    @pl.when(c == LAST)
    def _():
        for n in (24, 26, 28):
            greet(n, h)

    loads[2].wait()
    loads[3].wait()
    both = jnp.concatenate([ik[...].astype(F32), iv[...].astype(F32)], axis=0)
    outbox[...] = jnp.swapaxes(both, 0, 1).astype(BF16)
    loads[0].wait()
    loads[1].wait()
    keep_own = pltpu.make_async_copy(own, kv.at[ks(x, z, a)], keep.at[0])
    keep_own.start()

    pl.semaphore_wait(barrier, 14 + apart + 3 * (c // LAST))

    for d in range(1, HEADS):
        to = (h + d) % HEADS
        send(outbox.at[to], inbox.at[d], piece_s.at[d], piece_r.at[d], c, to)

    def halves(ref):
        return ref.at[pl.ds(0, 256)], ref.at[pl.ds(256, 256)]

    def along_x(i, n):
        dst = halves(kv.at[ks(x, order[i], a)])[n]
        src = halves(own)[n] if i == 0 else dst
        send(src, dst, xs.at[n, 0, i], xr.at[n, 0, i], ctx(right, z, a), h, x < 3)
        send(src, dst, xs.at[n, 1, i], xr.at[n, 1, i], ctx(left, z, a), h, x == 0 if i < 2 else x < 2)

    def share(kind, i, when=None):
        s = ks((x, left, right, far)[kind], order[i], a)
        src = own if (kind, i) == (0, 0) else kv.at[s]
        send(src, kv.at[s], sibs.at[kind, i], sibr.at[kind, i], ctx(x, z, 1 - a), h, when)

    def column(i):
        s = ks(x, order[i], a)
        arrived(kv.at[s], zr.at[order[i]])
        along_x(i, 0)
        along_x(i, 1)
        share(0, i)

    def from_left(i):
        for n, part in enumerate(halves(kv.at[ks(left, order[i], a)])):
            arrived(part, xr.at[n, 0, i], x > 0)
            if i < 2:
                send(part, part, rs.at[n, i], rr.at[n, i], ctx(right, z, a), h, x * (3 - x) > 0)
        share(1, i, x > 0)

    def from_right(i):
        for n, part in enumerate(halves(kv.at[ks(right, order[i], a)])):
            arrived(part, xr.at[n, 1, i], x == 3 if i < 2 else x * (3 - x) == 0)
            if i >= 2:
                send(part, part, rs.at[n, i], rr.at[n, i], ctx(left, z, a), h, x * (3 - x) == 0)
        share(2, i, x == 3)

    def from_far(i):
        for n, part in enumerate(halves(kv.at[ks(far, order[i], a)])):
            arrived(part, rr.at[n, i], x > 1)
        share(3, i, x > 1)

    conds = (None, x > 0, x == 3, x > 1)

    def other_core(kind, i):
        s = ks((x, left, right, far)[kind], order[i], 1 - a)
        arrived(kv.at[s], sibr.at[kind, i], conds[kind])

    def image_line(dz):
        part = img.at[pl.ds(si(0, (z + 4 - dz) % 4, a), 3)]
        if dz > 0:
            arrived(part, izr.at[dz])
        send(part, part, isibs.at[dz], isibr.at[dz], ctx(x, z, 1 - a), h)

    def block_bias(i, b):
        qb = 2 * c + i
        shown = jnp.where(b < qb, mask[qb, b], 0)
        return jnp.full((1, BLK), jnp.where(shown == 1, 0.0, HIDDEN), F32)

    def fill(kind, half):
        for u in range(2):
            for w in range(2):
                x_ = (x, left, right, far)[kind]
                core = a if w == 0 else 1 - a
                z_ = order[2 * half + u]
                s = ks(x_, z_, core)
                t = 4 * u + 2 * w
                keys[t * BLK:(t + 2) * BLK, :] = kv[s, :256, :]
                vals[t * BLK:(t + 2) * BLK, :128] = kv[s, 256:, :]
                for n in range(2):
                    for i in range(2):
                        bias[i, :, (t + n) * BLK:(t + n + 1) * BLK] = block_bias(
                            i, 2 * ctx(x_, z_, core) + n
                        )

    def work(kind, half, part=None):
        def extra(i, r):
            if (kind, half) != (0, 0):
                return bias[i]
            at = lax.broadcasted_iota(jnp.int32, (TILE, BLK), 0) // GROUP + r * (TILE // GROUP)
            key = lax.broadcasted_iota(jnp.int32, (TILE, BLK), 1)
            tri = jnp.where(key <= at, 0.0, HIDDEN)
            full = jnp.broadcast_to(bias[i], (TILE, SPAN * BLK))
            parts = [full[:, :i * BLK], tri, full[:, (i + 1) * BLK:]]
            return jnp.concatenate(parts[1 - min(i, 1):], axis=1)

        def go():
            if part != 1:
                fill(kind, half)
            for i in range(2):
                if part is None or part == i:
                    soft_step(q, keys, vals, acc, top, i * ROWS, functools.partial(extra, i))

        run(((None, z > 1), (x > 0,) * 2, (x == 3,) * 2, (x > 1,) * 2)[kind][half], go)

    s = ks(x, z, a)
    along_x(0, 0)
    along_x(0, 1)
    for i in range(1, 4):
        send(own, kv.at[s], zs.at[i], zr.at[z], ctx(x, order[i], a), h)
    share(0, 0)

    vals[:, 128:] = jnp.ones((SPAN * BLK, 128), BF16)
    top[...] = jnp.full_like(top, FLOOR)
    acc[...] = jnp.zeros_like(acc)
    loads[4].wait()
    loads[5].wait()
    keep_own.wait()

    column(1)
    from_left(0)
    from_right(0)

    inbox[0] = outbox[h]
    for d in range(1, HEADS):
        arrived(inbox.at[d], piece_r.at[d])
    rows = inbox[...].astype(F32)
    si_mine = si(x, z, a)
    own_img[:64] = rows[:, :8, :].reshape(64, 128).astype(BF16)
    own_img[64:] = rows[:, 8:, :].reshape(64, 128).astype(BF16)
    keep_img = pltpu.make_async_copy(own_img, img.at[si_mine], keep.at[1])
    keep_img.start()
    for d, x_ in ((1, right), (2, far), (3, left)):
        send(own_img, img.at[si_mine], ixs.at[d], ixr.at[d], ctx(x_, z, a), h, x < 3)
    nth = jnp.minimum(jnp.maximum(c - 24, 0), 6)
    send(own_img, img.at[si_mine], last_s.at[0], last_r.at[nth], LAST, h, final)

    other_core(0, 0)
    other_core(0, 1)
    work(0, 0, 0)
    column(2)
    from_left(1)
    from_right(1)
    work(0, 0, 1)
    column(3)
    for d, x_ in ((1, left), (2, far), (3, right)):
        arrived(img.at[si(x_, z, a)], ixr.at[d], (x + 4 - d) % 4 < 3)
    keep_img.wait()
    part = img.at[pl.ds(si(0, z, a), 3)]
    for dz in (1, 3, 2):
        send(part, part, izs.at[dz], izr.at[dz], ctx(x, (z + dz) % 4, a), h)
    image_line(0)
    other_core(1, 0)
    other_core(1, 1)
    work(1, 0, 0)
    from_right(2)
    from_left(2)
    work(1, 0, 1)
    from_right(3)
    from_left(3)
    other_core(2, 0)
    other_core(2, 1)
    from_far(0)
    work(2, 0)
    from_far(1)
    image_line(1)
    other_core(0, 2)
    other_core(0, 3)
    image_line(3)
    from_far(2)
    work(0, 1)
    image_line(2)
    other_core(3, 0)
    other_core(3, 1)
    work(3, 0)
    from_far(3)
    for kind in (1, 2, 3):
        other_core(kind, 2)
        other_core(kind, 3)
        if (kind, 1) not in LATER:
            work(kind, 1)
    for i in range(4):
        part = img.at[pl.ds(si(0, (z + 4 - i) % 4, 1 - a), 3)]
        arrived(part, isibr.at[i])
    for n in range(7):
        block = img.at[si(3, n // 2, n % 2)]
        arrived(block, last_r.at[n], c == LAST)
    for when, done in pending:
        run(when, done)


def attend_kernel(
    offsets_hbm, first_hbm, mask_hbm, q_hbm, kv, img, acc, top, self_hbm, cross_hbm,
    q, keys, vals, acc2, top2, bias, out, seen, offsets, first, mask, sems,
):
    c = lax.axis_index("ctx")
    x, z = c // 8, (c // 2) % 4
    loads = [
        pltpu.make_async_copy(src, dst, sems.at[n])
        for n, (src, dst) in enumerate((
            (mask_hbm, mask), (offsets_hbm, offsets), (first_hbm, first), (q_hbm, q),
        ))
    ]
    for load in loads:
        load.start()
    vals[:, :, 128:] = jnp.ones((2, SPAN * BLK, 128), BF16)
    top2[...] = jnp.full_like(top2, FLOOR)
    acc2[...] = jnp.zeros_like(acc2)
    for load in loads:
        load.wait()

    def result(a_ref):
        total = a_ref[:, 128:]
        good = total > 0.0
        return jnp.where(good, a_ref[:, :128] / jnp.where(good, total, 1.0), 0.0).astype(BF16)

    def cross(i, pair):
        qb = 2 * c + i
        both = (2 * pair, 2 * pair + 1)
        lowest = [jnp.where(m >= first[qb], offsets[m], 1 << 30) for m in both]
        last = qb * BLK + BLK - 1

        @pl.when((lowest[0] <= last) | (lowest[1] <= last))
        def _():
            for n, m in enumerate(both):
                for d in range(8):
                    held = jnp.where(c == LAST, m, m - 1) if m == IMAGES - 1 else m
                    s = (d % 2) * 16 + (d // 2) * 4 + held
                    row = n * IMG_LEN + d * 64
                    keys[i, row:row + 64, :] = img[s, :64, :]
                    vals[i, row:row + 64, :128] = img[s, 64:, :]

            def extra(r):
                at = lax.broadcasted_iota(jnp.int32, (TILE, IMG_LEN), 0) // GROUP + (
                    r * (TILE // GROUP) + qb * BLK
                )
                return jnp.concatenate(
                    [jnp.where(at >= low, 0.0, HIDDEN) for low in lowest], axis=1
                )

            soft_step(q, keys.at[i], vals.at[i], acc2, top2, i * ROWS, extra)

    for pair in range(2):
        for i in range(2):
            cross(i, pair)
    out[1] = result(acc2)
    put_cross = pltpu.make_async_copy(out.at[1], cross_hbm, sems.at[4])
    put_cross.start()

    counts = []
    for i in range(2):
        qb = 2 * c + i
        n = jnp.int32(0)
        for kind, half in LATER:
            x_ = (x + 1) % 4 if kind == 2 else (x + 2) % 4
            there = (x == 3) if kind == 2 else (x > 1)
            for u in range(2):
                z_ = 2 - z // 2 if u == 0 else 3 - 3 * (z // 2)
                for w in range(4):
                    b = jnp.where(there, x_ * 16 + z_ * 4 + w, 0)
                    seen[i, n] = b
                    n = n + jnp.where(there, mask[qb, b], 0)
        counts.append(n)

    def span(j, _):
        for i in range(2):
            for t in range(SPAN):
                n = j * SPAN + t
                live = n < counts[i]
                b = jnp.where(live, seen[i, jnp.where(live, n, 0)], 2 * c)
                dev = b // 2
                s = (dev % 2) * 16 + (dev // 8) * 4 + (dev // 2) % 4
                half = pl.multiple_of((b % 2) * BLK, BLK)
                keys[i, t * BLK:(t + 1) * BLK, :] = kv[s, pl.ds(half, BLK), :]
                vals[i, t * BLK:(t + 1) * BLK, :128] = kv[s, pl.ds(256 + half, BLK), :]
                bias[i, :, t * BLK:(t + 1) * BLK] = jnp.full(
                    (1, BLK), jnp.where(live, 0.0, HIDDEN), F32
                )
        for i in range(2):
            soft_step(q, keys.at[i], vals.at[i], acc, top, i * ROWS, lambda r: bias[i])
        return 0

    steps = (jnp.maximum(counts[0], counts[1]) + SPAN - 1) // SPAN
    lax.fori_loop(0, steps, span, 0)
    out[0] = result(acc)
    put_self = pltpu.make_async_copy(out.at[0], self_hbm, sems.at[5])
    put_self.start()
    put_cross.wait()
    put_self.wait()


def attend_call(offsets, first, mask, q, kv, img, acc, top):
    vmem = pl.BlockSpec(memory_space=pltpu.VMEM)
    hbm = pl.BlockSpec(memory_space=pltpu.HBM)
    n = q.shape[0]
    return pl.pallas_call(
        attend_kernel,
        out_shape=(jax.ShapeDtypeStruct((n, 128), BF16),) * 2,
        in_specs=[hbm] * 4 + [vmem] * 4,
        out_specs=(hbm, hbm),
        scratch_shapes=[
            pltpu.VMEM((n, 128), BF16),
            pltpu.VMEM((2, SPAN * BLK, 128), BF16),
            pltpu.VMEM((2, SPAN * BLK, 256), BF16),
            pltpu.VMEM((n, 256), F32),
            pltpu.VMEM((n, 128), F32),
            pltpu.VMEM((2, 1, SPAN * BLK), F32),
            pltpu.VMEM((2, n, 128), BF16),
            pltpu.SMEM((2, 64), jnp.int32),
            pltpu.SMEM((IMAGES,), jnp.int32),
            pltpu.SMEM(first.shape, jnp.int32),
            pltpu.SMEM(mask.shape, jnp.int32),
            pltpu.SemaphoreType.DMA((6,)),
        ],
        compiler_params=pltpu.CompilerParams(vmem_limit_bytes=32 * 2**20),
    )(*[pltpu.with_memory_space_constraint(t, pltpu.HBM) for t in (offsets, first, mask, q)], kv, img, acc, top)


def gather_call(q, k, v, ik, iv, mask):
    vmem = pl.BlockSpec(memory_space=pltpu.VMEM)
    hbm = pl.BlockSpec(memory_space=pltpu.HBM)
    dma = pltpu.SemaphoreType.DMA
    n = q.shape[0] * q.shape[1]
    rows = q.reshape(n, 128)
    return pl.pallas_call(
        gather_kernel,
        out_shape=(
            jax.ShapeDtypeStruct((32, 512, 128), BF16),
            jax.ShapeDtypeStruct((32, 128, 128), BF16),
            jax.ShapeDtypeStruct((n, 256), F32),
            jax.ShapeDtypeStruct((n, 128), F32),
        ),
        in_specs=[hbm] * 6,
        out_specs=(vmem,) * 4,
        scratch_shapes=[
            pltpu.VMEM((512, 128), BF16),
            pltpu.VMEM((128, 128), BF16),
            pltpu.VMEM((8, 16, 128), BF16),
            pltpu.VMEM((8, 16, 128), BF16),
            pltpu.VMEM((8, 8, 128), BF16),
            pltpu.VMEM((8, 8, 128), BF16),
            pltpu.VMEM((n, 128), BF16),
            pltpu.SMEM(mask.shape, jnp.int32),
            pltpu.VMEM((SPAN * BLK, 128), BF16),
            pltpu.VMEM((SPAN * BLK, 256), BF16),
            pltpu.VMEM((2, 1, SPAN * BLK), F32),
            dma((8,)), dma((8,)),
            dma((4,)), dma((4,)),
            dma((2, 2, 4)), dma((2, 2, 4)),
            dma((2, 4)), dma((2, 4)),
            dma((4, 4)), dma((4, 4)),
            dma((4,)), dma((4,)),
            dma((4,)), dma((4,)),
            dma((4,)), dma((4,)),
            dma((1,)), dma((7,)),
            dma((8,)),
        ],
        compiler_params=pltpu.CompilerParams(
            collective_id=0, has_side_effects=True, vmem_limit_bytes=32 * 2**20
        ),
    )(*[pltpu.with_memory_space_constraint(t, pltpu.HBM) for t in (k.reshape(-1, 128), v.reshape(-1, 128), ik, iv, rows, mask)])


def per_device(q, k, v, ik, iv, offsets, first, mask):
    kv, img, acc, top = gather_call(q, k, v, ik, iv, mask)
    rows = q.reshape(-1, 128)
    self_out, cross_out = attend_call(offsets, first, mask, rows, kv, img, acc, top)
    return self_out.reshape(q.shape), cross_out.reshape(q.shape)


def solution(mesh):
    return jax.shard_map(
        per_device,
        mesh=mesh,
        in_specs=(
            P("ctx", "head", None),
            P("ctx", "head", None),
            P("ctx", "head", None),
            P(("ctx", "head"), None, None),
            P(("ctx", "head"), None, None),
            P(),
            P(),
            P(),
        ),
        out_specs=(P("ctx", "head", None), P("ctx", "head", None)),
        check_vma=False,
    )
```

```python
import functools
import math

import jax
import jax.numpy as jnp
from jax import lax
from jax.experimental import pallas as pl
from jax.experimental.pallas import tpu as pltpu
from jax.sharding import PartitionSpec as P

MESH = pl.DeviceIdType.MESH
BF16 = jnp.bfloat16
F32 = jnp.float32

HEADS = 8
XS, ZS = 4, 4
BLK = 128
GROUP = 8
ROWS = BLK * GROUP
IMAGES = 4
IMG_LEN = 512
TILE = 128
SPAN = 8
LATER = ((1, 1), (2, 1), (3, 1))
LAST = 31
LOG2E = 1.4426950408889634
HIDDEN = -1e30
FLOOR = -1e28


def soft_step(q_ref, keys, vals, acc, top, first_row, extra):
    scale = LOG2E / math.sqrt(128.0)
    for r in range(ROWS // TILE):
        here = pl.ds(first_row + r * TILE, TILE)
        scores = lax.dot_general(
            q_ref[here, :], keys[...], (((1,), (1,)), ((), ())), preferred_element_type=F32
        )
        scores = scores + extra(r)
        old = top[here, :]
        new = jnp.maximum(old, jnp.max(scores, axis=1, keepdims=True))
        top[here, :] = new
        weights = jnp.exp2((scores - new[:, :1]) * scale).astype(BF16)
        shrink = jnp.exp2((old - new) * scale)
        shrink = jnp.concatenate([shrink, shrink], axis=1)
        acc[here, :] = acc[here, :] * shrink + jnp.dot(
            weights, vals[...], preferred_element_type=F32
        )


def gather_kernel(
    k_hbm, v_hbm, ik_hbm, iv_hbm, q_hbm, mask_hbm, kv, img, acc, top,
    own, own_img, outbox, inbox, ik, iv, q, mask, keys, vals, bias,
    piece_s, piece_r, zs, zr, xs, xr, rs, rr, sibs, sibr, ixs, ixr, izs, izr, isibs, isibr, last_s, last_r, keep,
):
    c = lax.axis_index("ctx")
    h = lax.axis_index("head")
    x, z, a = c // 8, (c // 2) % 4, c % 2
    left, right, far = (x + 3) % 4, (x + 1) % 4, (x + 2) % 4
    order = (z, z + 1 - 2 * (z % 2), 2 - z // 2, 3 - 3 * (z // 2))
    final = (c // 24) * (31 - c) > 0

    def ctx(x_, z_, a_):
        return x_ * 8 + z_ * 2 + a_

    def ks(x_, z_, a_):
        return a_ * 16 + x_ * 4 + z_

    def si(x_, z_, a_):
        return a_ * 16 + z_ * 4 + x_

    def rcopy(src, dst, ssem, rsem, to_ctx, to_head):
        return pltpu.make_async_remote_copy(
            src_ref=src, dst_ref=dst, send_sem=ssem, recv_sem=rsem,
            device_id=(to_ctx, to_head), device_id_type=MESH,
        )

    pending = []

    def run(when, go):
        if when is None:
            go()
        else:
            pl.when(when)(go)

    def send(src, dst, ssem, rsem, to_ctx, to_head, when=None):
        run(when, lambda: rcopy(src, dst, ssem, rsem, to_ctx, to_head).start())
        pending.append(
            (when, lambda: rcopy(src, dst, ssem, rsem, to_ctx, to_head).wait_send())
        )

    def arrived(dst, rsem, when=None):
        run(when, lambda: rcopy(dst, dst, rsem, rsem, ctx(x, z, 1 - a), h).wait_recv())

    loads = [
        pltpu.make_async_copy(src, dst, keep.at[2 + n])
        for n, (src, dst) in enumerate((
            (k_hbm, own.at[pl.ds(0, 256)]), (v_hbm, own.at[pl.ds(256, 256)]),
            (ik_hbm, ik), (iv_hbm, iv), (q_hbm, q), (mask_hbm, mask),
        ))
    ]
    for load in loads:
        load.start()

    barrier = pltpu.get_barrier_semaphore()

    def greet(to_ctx, to_head):
        pl.semaphore_signal(barrier, inc=1, device_id=(to_ctx, to_head), device_id_type=MESH)

    for d in range(1, HEADS):
        greet(c, (h + d) % HEADS)
    greet(ctx(x, z, 1 - a), h)
    for x_ in (left, right, far):
        greet(ctx(x_, z, a), h)
    for dz in range(1, 4):
        greet(ctx(x, (z + dz) % 4, a), h)
    apart = (c // 24) * (1 - c // 29) * (1 - a)
    pl.when(apart > 0)(lambda: greet(LAST, h))

    @pl.when(c == LAST)
    def _():
        for n in (24, 26, 28):
            greet(n, h)

    loads[2].wait()
    loads[3].wait()
    both = jnp.concatenate([ik[...].astype(F32), iv[...].astype(F32)], axis=0)
    outbox[...] = jnp.swapaxes(both, 0, 1).astype(BF16)
    loads[0].wait()
    loads[1].wait()
    keep_own = pltpu.make_async_copy(own, kv.at[ks(x, z, a)], keep.at[0])
    keep_own.start()

    pl.semaphore_wait(barrier, 14 + apart + 3 * (c // LAST))

    for d in range(1, HEADS):
        to = (h + d) % HEADS
        send(outbox.at[to], inbox.at[d], piece_s.at[d], piece_r.at[d], c, to)

    def halves(ref):
        return ref.at[pl.ds(0, 256)], ref.at[pl.ds(256, 256)]

    def along_x(i, n):
        dst = halves(kv.at[ks(x, order[i], a)])[n]
        src = halves(own)[n] if i == 0 else dst
        send(src, dst, xs.at[n, 0, i], xr.at[n, 0, i], ctx(right, z, a), h, x < 3)
        send(src, dst, xs.at[n, 1, i], xr.at[n, 1, i], ctx(left, z, a), h, x == 0 if i < 2 else x < 2)

    def share(kind, i, when=None):
        s = ks((x, left, right, far)[kind], order[i], a)
        src = own if (kind, i) == (0, 0) else kv.at[s]
        send(src, kv.at[s], sibs.at[kind, i], sibr.at[kind, i], ctx(x, z, 1 - a), h, when)

    def column(i):
        s = ks(x, order[i], a)
        arrived(kv.at[s], zr.at[order[i]])
        along_x(i, 0)
        along_x(i, 1)
        share(0, i)

    def from_left(i):
        for n, part in enumerate(halves(kv.at[ks(left, order[i], a)])):
            arrived(part, xr.at[n, 0, i], x > 0)
            if i < 2:
                send(part, part, rs.at[n, i], rr.at[n, i], ctx(right, z, a), h, x * (3 - x) > 0)
        share(1, i, x > 0)

    def from_right(i):
        for n, part in enumerate(halves(kv.at[ks(right, order[i], a)])):
            arrived(part, xr.at[n, 1, i], x == 3 if i < 2 else x * (3 - x) == 0)
            if i >= 2:
                send(part, part, rs.at[n, i], rr.at[n, i], ctx(left, z, a), h, x * (3 - x) == 0)
        share(2, i, x == 3)

    def from_far(i):
        for n, part in enumerate(halves(kv.at[ks(far, order[i], a)])):
            arrived(part, rr.at[n, i], x > 1)
        share(3, i, x > 1)

    conds = (None, x > 0, x == 3, x > 1)

    def other_core(kind, i):
        s = ks((x, left, right, far)[kind], order[i], 1 - a)
        arrived(kv.at[s], sibr.at[kind, i], conds[kind])

    def image_line(dz):
        part = img.at[pl.ds(si(0, (z + 4 - dz) % 4, a), 3)]
        if dz > 0:
            arrived(part, izr.at[dz])
        send(part, part, isibs.at[dz], isibr.at[dz], ctx(x, z, 1 - a), h)

    def block_bias(i, b):
        qb = 2 * c + i
        shown = jnp.where(b < qb, mask[qb, b], 0)
        return jnp.full((1, BLK), jnp.where(shown == 1, 0.0, HIDDEN), F32)

    def fill(kind, half):
        for u in range(2):
            for w in range(2):
                x_ = (x, left, right, far)[kind]
                core = a if w == 0 else 1 - a
                z_ = order[2 * half + u]
                s = ks(x_, z_, core)
                t = 4 * u + 2 * w
                keys[t * BLK:(t + 2) * BLK, :] = kv[s, :256, :]
                vals[t * BLK:(t + 2) * BLK, :128] = kv[s, 256:, :]
                for n in range(2):
                    for i in range(2):
                        bias[i, :, (t + n) * BLK:(t + n + 1) * BLK] = block_bias(
                            i, 2 * ctx(x_, z_, core) + n
                        )

    def work(kind, half, part=None):
        def extra(i, r):
            if (kind, half) != (0, 0):
                return bias[i]
            at = lax.broadcasted_iota(jnp.int32, (TILE, BLK), 0) // GROUP + r * (TILE // GROUP)
            key = lax.broadcasted_iota(jnp.int32, (TILE, BLK), 1)
            tri = jnp.where(key <= at, 0.0, HIDDEN)
            full = jnp.broadcast_to(bias[i], (TILE, SPAN * BLK))
            parts = [full[:, :i * BLK], tri, full[:, (i + 1) * BLK:]]
            return jnp.concatenate(parts[1 - min(i, 1):], axis=1)

        def go():
            if part != 1:
                fill(kind, half)
            for i in range(2):
                if part is None or part == i:
                    soft_step(q, keys, vals, acc, top, i * ROWS, functools.partial(extra, i))

        run(((None, z > 1), (x > 0,) * 2, (x == 3,) * 2, (x > 1,) * 2)[kind][half], go)

    s = ks(x, z, a)
    along_x(0, 0)
    along_x(0, 1)
    for i in range(1, 4):
        send(own, kv.at[s], zs.at[i], zr.at[z], ctx(x, order[i], a), h)
    share(0, 0)

    vals[:, 128:] = jnp.ones((SPAN * BLK, 128), BF16)
    top[...] = jnp.full_like(top, FLOOR)
    acc[...] = jnp.zeros_like(acc)
    loads[4].wait()
    loads[5].wait()
    keep_own.wait()

    column(1)
    from_left(0)
    from_right(0)

    inbox[0] = outbox[h]
    for d in range(1, HEADS):
        arrived(inbox.at[d], piece_r.at[d])
    rows = inbox[...].astype(F32)
    si_mine = si(x, z, a)
    own_img[:64] = rows[:, :8, :].reshape(64, 128).astype(BF16)
    own_img[64:] = rows[:, 8:, :].reshape(64, 128).astype(BF16)
    keep_img = pltpu.make_async_copy(own_img, img.at[si_mine], keep.at[1])
    keep_img.start()
    for d, x_ in ((1, right), (2, far), (3, left)):
        send(own_img, img.at[si_mine], ixs.at[d], ixr.at[d], ctx(x_, z, a), h, x < 3)
    nth = jnp.minimum(jnp.maximum(c - 24, 0), 6)
    send(own_img, img.at[si_mine], last_s.at[0], last_r.at[nth], LAST, h, final)

    other_core(0, 0)
    other_core(0, 1)
    work(0, 0, 0)
    column(2)
    from_left(1)
    from_right(1)
    for d, x_ in ((1, left), (2, far), (3, right)):
        arrived(img.at[si(x_, z, a)], ixr.at[d], (x + 4 - d) % 4 < 3)
    keep_img.wait()
    part = img.at[pl.ds(si(0, z, a), 3)]
    for dz in (1, 3, 2):
        send(part, part, izs.at[dz], izr.at[dz], ctx(x, (z + dz) % 4, a), h)
    image_line(0)
    work(0, 0, 1)
    column(3)
    other_core(1, 0)
    other_core(1, 1)
    from_right(2)
    from_left(2)
    work(1, 0)
    from_right(3)
    from_left(3)
    other_core(2, 0)
    other_core(2, 1)
    from_far(0)
    work(2, 0)
    from_far(1)
    image_line(1)
    other_core(3, 0)
    other_core(3, 1)
    work(3, 0)
    from_far(2)
    image_line(3)
    other_core(1, 2)
    other_core(1, 3)
    if (1, 1) not in LATER:
        work(1, 1)
    from_far(3)
    image_line(2)
    other_core(0, 2)
    other_core(0, 3)
    if (0, 1) not in LATER:
        work(0, 1)
    other_core(2, 2)
    other_core(2, 3)
    if (2, 1) not in LATER:
        work(2, 1)
    other_core(3, 2)
    other_core(3, 3)
    for i in range(4):
        part = img.at[pl.ds(si(0, (z + 4 - i) % 4, 1 - a), 3)]
        arrived(part, isibr.at[i])
    for n in range(7):
        block = img.at[si(3, n // 2, n % 2)]
        arrived(block, last_r.at[n], c == LAST)
    for when, done in pending:
        run(when, done)


def attend_kernel(
    offsets_hbm, first_hbm, mask_hbm, q_hbm, kv, img, acc, top, self_hbm, cross_hbm,
    q, keys, vals, acc2, top2, bias, out, seen, offsets, first, mask, sems,
):
    c = lax.axis_index("ctx")
    x, z = c // 8, (c // 2) % 4
    loads = [
        pltpu.make_async_copy(src, dst, sems.at[n])
        for n, (src, dst) in enumerate((
            (mask_hbm, mask), (offsets_hbm, offsets), (first_hbm, first), (q_hbm, q),
        ))
    ]
    for load in loads:
        load.start()
    vals[:, :, 128:] = jnp.ones((2, SPAN * BLK, 128), BF16)
    top2[...] = jnp.full_like(top2, FLOOR)
    acc2[...] = jnp.zeros_like(acc2)
    for load in loads:
        load.wait()

    def result(a_ref):
        total = a_ref[:, 128:]
        good = total > 0.0
        return jnp.where(good, a_ref[:, :128] / jnp.where(good, total, 1.0), 0.0).astype(BF16)

    def cross(i, pair):
        qb = 2 * c + i
        both = (2 * pair, 2 * pair + 1)
        lowest = [jnp.where(m >= first[qb], offsets[m], 1 << 30) for m in both]
        last = qb * BLK + BLK - 1

        @pl.when((lowest[0] <= last) | (lowest[1] <= last))
        def _():
            for n, m in enumerate(both):
                for d in range(8):
                    held = jnp.where(c == LAST, m, m - 1) if m == IMAGES - 1 else m
                    s = (d % 2) * 16 + (d // 2) * 4 + held
                    row = n * IMG_LEN + d * 64
                    keys[i, row:row + 64, :] = img[s, :64, :]
                    vals[i, row:row + 64, :128] = img[s, 64:, :]

            def extra(r):
                at = lax.broadcasted_iota(jnp.int32, (TILE, BLK), 0) // GROUP + (
                    r * (TILE // GROUP) + qb * BLK
                )
                return jnp.concatenate(
                    [jnp.where(at >= low, 0.0, HIDDEN) for low in lowest for _ in range(IMG_LEN // BLK)], axis=1
                )

            soft_step(q, keys.at[i], vals.at[i], acc2, top2, i * ROWS, extra)

    for pair in range(2):
        for i in range(2):
            cross(i, pair)
    out[1] = result(acc2)
    put_cross = pltpu.make_async_copy(out.at[1], cross_hbm, sems.at[4])
    put_cross.start()

    counts = []
    for i in range(2):
        qb = 2 * c + i
        n = jnp.int32(0)
        for kind, half in LATER:
            x_ = (x, (x + 3) % 4, (x + 1) % 4, (x + 2) % 4)[kind]
            there = (z > 1, x > 0, x == 3, x > 1)[kind]
            for u in range(2):
                z_ = 2 - z // 2 if u == 0 else 3 - 3 * (z // 2)
                for w in range(4):
                    b = jnp.where(there, x_ * 16 + z_ * 4 + w, 0)
                    seen[i, n] = b
                    n = n + jnp.where(there, mask[qb, b], 0)
        counts.append(n)

    def span(first_n, width):
        for i in range(2):
            for t in range(width):
                n = first_n + t
                live = n < counts[i]
                b = jnp.where(live, seen[i, jnp.where(live, n, 0)], 2 * c)
                dev = b // 2
                s = (dev % 2) * 16 + (dev // 8) * 4 + (dev // 2) % 4
                half = pl.multiple_of((b % 2) * BLK, BLK)
                keys[i, t * BLK:(t + 1) * BLK, :] = kv[s, pl.ds(half, BLK), :]
                vals[i, t * BLK:(t + 1) * BLK, :128] = kv[s, pl.ds(256 + half, BLK), :]
                bias[i, :, t * BLK:(t + 1) * BLK] = jnp.full(
                    (1, BLK), jnp.where(live, 0.0, HIDDEN), F32
                )
        wide = pl.ds(0, width * BLK)
        for i in range(2):
            soft_step(
                q, keys.at[i, wide], vals.at[i, wide], acc, top, i * ROWS,
                lambda r: bias[i, :, :width * BLK],
            )

    most = jnp.maximum(counts[0], counts[1])
    steps = (most + SPAN // 2 - 1) // SPAN

    def one_span(j, carry):
        span(j * SPAN, SPAN)
        return carry

    lax.fori_loop(0, steps, one_span, 0)
    pl.when(most > steps * SPAN)(lambda: span(steps * SPAN, SPAN // 2))
    out[0] = result(acc)
    put_self = pltpu.make_async_copy(out.at[0], self_hbm, sems.at[5])
    put_self.start()
    put_cross.wait()
    put_self.wait()


def attend_call(offsets, first, mask, q, kv, img, acc, top):
    vmem = pl.BlockSpec(memory_space=pltpu.VMEM)
    hbm = pl.BlockSpec(memory_space=pltpu.HBM)
    n = q.shape[0]
    return pl.pallas_call(
        attend_kernel,
        out_shape=(jax.ShapeDtypeStruct((n, 128), BF16),) * 2,
        in_specs=[hbm] * 4 + [vmem] * 4,
        out_specs=(hbm, hbm),
        scratch_shapes=[
            pltpu.VMEM((n, 128), BF16),
            pltpu.VMEM((2, SPAN * BLK, 128), BF16),
            pltpu.VMEM((2, SPAN * BLK, 256), BF16),
            pltpu.VMEM((n, 256), F32),
            pltpu.VMEM((n, 128), F32),
            pltpu.VMEM((2, 1, SPAN * BLK), F32),
            pltpu.VMEM((2, n, 128), BF16),
            pltpu.SMEM((2, 64), jnp.int32),
            pltpu.SMEM((IMAGES,), jnp.int32),
            pltpu.SMEM(first.shape, jnp.int32),
            pltpu.SMEM(mask.shape, jnp.int32),
            pltpu.SemaphoreType.DMA((6,)),
        ],
        compiler_params=pltpu.CompilerParams(vmem_limit_bytes=32 * 2**20),
    )(*[pltpu.with_memory_space_constraint(t, pltpu.HBM) for t in (offsets, first, mask, q)], kv, img, acc, top)


def gather_call(q, k, v, ik, iv, mask):
    vmem = pl.BlockSpec(memory_space=pltpu.VMEM)
    hbm = pl.BlockSpec(memory_space=pltpu.HBM)
    dma = pltpu.SemaphoreType.DMA
    n = q.shape[0] * q.shape[1]
    rows = q.reshape(n, 128)
    return pl.pallas_call(
        gather_kernel,
        out_shape=(
            jax.ShapeDtypeStruct((32, 512, 128), BF16),
            jax.ShapeDtypeStruct((32, 128, 128), BF16),
            jax.ShapeDtypeStruct((n, 256), F32),
            jax.ShapeDtypeStruct((n, 128), F32),
        ),
        in_specs=[hbm] * 6,
        out_specs=(vmem,) * 4,
        scratch_shapes=[
            pltpu.VMEM((512, 128), BF16),
            pltpu.VMEM((128, 128), BF16),
            pltpu.VMEM((8, 16, 128), BF16),
            pltpu.VMEM((8, 16, 128), BF16),
            pltpu.VMEM((8, 8, 128), BF16),
            pltpu.VMEM((8, 8, 128), BF16),
            pltpu.VMEM((n, 128), BF16),
            pltpu.SMEM(mask.shape, jnp.int32),
            pltpu.VMEM((SPAN * BLK, 128), BF16),
            pltpu.VMEM((SPAN * BLK, 256), BF16),
            pltpu.VMEM((2, 1, SPAN * BLK), F32),
            dma((8,)), dma((8,)),
            dma((4,)), dma((4,)),
            dma((2, 2, 4)), dma((2, 2, 4)),
            dma((2, 4)), dma((2, 4)),
            dma((4, 4)), dma((4, 4)),
            dma((4,)), dma((4,)),
            dma((4,)), dma((4,)),
            dma((4,)), dma((4,)),
            dma((1,)), dma((7,)),
            dma((8,)),
        ],
        compiler_params=pltpu.CompilerParams(
            collective_id=0, has_side_effects=True, vmem_limit_bytes=32 * 2**20
        ),
    )(*[pltpu.with_memory_space_constraint(t, pltpu.HBM) for t in (k.reshape(-1, 128), v.reshape(-1, 128), ik, iv, rows, mask)])


def per_device(q, k, v, ik, iv, offsets, first, mask):
    kv, img, acc, top = gather_call(q, k, v, ik, iv, mask)
    rows = q.reshape(-1, 128)
    self_out, cross_out = attend_call(offsets, first, mask, rows, kv, img, acc, top)
    return self_out.reshape(q.shape), cross_out.reshape(q.shape)


def solution(mesh):
    return jax.shard_map(
        per_device,
        mesh=mesh,
        in_specs=(
            P("ctx", "head", None),
            P("ctx", "head", None),
            P("ctx", "head", None),
            P(("ctx", "head"), None, None),
            P(("ctx", "head"), None, None),
            P(),
            P(),
            P(),
        ),
        out_specs=(P("ctx", "head", None), P("ctx", "head", None)),
        check_vma=False,
    )
```
